32 devices in a mesh: groups: 2 (over y), ffn: 4 (over z), mp: 4 (over x, core).
Axes of the slice: x: 2, y: 2, z: 4, core: 2. Of those that a mesh axis runs over, the one named last changes fastest.
Arguments:
- tokens: bfloat16 [64, 8192], P(('groups', 'ffn'), 'mp'), parts along dimension 0, may hold values from -6 to 6
- gate_weight: bfloat16 [8192, 26624], P('mp', 'ffn'), may hold values from -0.0625 to 0.0625
- up_weight: bfloat16 [8192, 26624], P('mp', 'ffn'), may hold values from -0.0625 to 0.0625
- down_weight: bfloat16 [26624, 8192], P('ffn', 'mp'), may hold values from -0.0390625 to 0.0390625
Outputs:
- block_out: bfloat16 [64, 8192], P(('groups', 'ffn'), 'mp'), parts along dimension 0
The draws below stay inside these ranges and needn't reach their ends.
There are 2 independent parts, one for each index of `groups`. The reference program is written for one: setup_inputs(seed, part) draws one part's arguments, and reference() takes and returns one part's arrays. A program takes and returns all parts, laid end to end along the dimension named above; an argument that names none is the same for every part. Nothing has to cross between parts.
All inputs are finite; a program needn't handle non-finite values.
Results may differ from the reference program's by a relative error of at most 0.0049.
Values may be sent and summed in bfloat16 or wider, within the bound.
No kernel may reach another device: no remote copies, remote signals or barrier semaphores. Data moves between devices by JAX's collectives and lax.ppermute only.
A program may use at most 192 MiB of HBM per device.

```python
import jax
import jax.numpy as jnp

D = 8192
FF = 26624
ROWS = 32


def steps_of(key, shape, pieces, smallest, largest):
    def one(axis_at, parts):
        heights = jax.random.uniform(jax.random.fold_in(jax.random.fold_in(key, 6), axis_at), (parts,), jnp.float32, smallest / len(pieces), largest / len(pieces))
        return jnp.repeat(jnp.exp(heights), shape[axis_at] // parts).reshape((-1,) + (1,) * (len(shape) - axis_at - 1))

    factor_of = one(*pieces[0])
    for cut in pieces[1:]:
        factor_of = factor_of * one(*cut)
    return factor_of


def bell_draw(own_key, shape, width, bound, pieces=(), kind=jnp.bfloat16):
    loudness = steps_of(own_key, shape, pieces, -0.22, 0.18) if pieces else 1.0
    drawn = jax.random.normal(own_key, shape, jnp.float32) * width * loudness
    return jnp.minimum(jnp.maximum(drawn, -bound), bound).astype(kind)


def setup_inputs(seed: int = 0, part: int = 0) -> dict:
    splits = jax.random.split(jax.random.key(seed), 5)
    part_splits = jax.random.split(jax.random.fold_in(splits[4], part), 5)
    tokens = bell_draw(part_splits[0], (ROWS, D), 1.0, 6.0, ((0, 4), (1, 4)))
    gate_weight = bell_draw(splits[1], (D, FF), D ** -0.5, 0.0625, ((0, 4), (1, 4)))
    up_weight = bell_draw(splits[2], (D, FF), D ** -0.5, 0.0625, ((0, 4), (1, 4)))
    down_weight = bell_draw(splits[3], (FF, D), FF ** -0.5, 0.0390625, ((0, 4), (1, 4)))
    return {"tokens": tokens, "gate_weight": gate_weight, "up_weight": up_weight, "down_weight": down_weight}


def reference(tokens, gate_weight, up_weight, down_weight):
    gate = jnp.dot(tokens, gate_weight, preferred_element_type=jnp.float32)
    up = jnp.dot(tokens, up_weight, preferred_element_type=jnp.float32)
    hidden = (jax.nn.silu(gate) * up).astype(jnp.bfloat16)
    return jnp.dot(hidden, down_weight, preferred_element_type=jnp.float32).astype(jnp.bfloat16)
```

```python
import jax
import jax.numpy as jnp
from jax import lax
from jax.experimental import pallas as pl
from jax.experimental.pallas import tpu as pltpu
from jax.sharding import PartitionSpec as P

BF16 = jnp.bfloat16
F32 = jnp.float32
VMEM = pl.BlockSpec(memory_space=pltpu.VMEM)
ANY = pl.BlockSpec(memory_space=pl.ANY)
COST = pl.CostEstimate(flops=1000, bytes_accessed=1000, transcendentals=0)


def in_hbm(array):
    return pltpu.with_memory_space_constraint(array, pltpu.HBM)


def flip(size, bit):
    return [(i, i ^ bit) for i in range(size)]


def step(name, body, ins, outs, fetches, deps=()):
    n_in, n_out, n_fetch = len(ins), len(outs), len(fetches)
    n_sems = sum(pieces for *_, pieces in fetches)

    def kernel(*refs):
        in_refs, refs = refs[:n_in], refs[n_in:]
        sources, refs = refs[:n_fetch], refs[n_fetch + len(deps) :]
        out_refs, refs = refs[:n_out], refs[n_out:]
        targets, refs = refs[:n_fetch], refs[n_fetch:]
        core = lax.rem(lax.axis_index("mp"), 2)
        copies = []
        for (_, height, width, place, pieces), source, target in zip(fetches, sources, targets):
            row, column = place(core)
            tall = height // pieces
            for i in range(pieces):
                copies.append(
                    pltpu.make_async_copy(
                        source.at[
                            pl.ds(pl.multiple_of(row + i * tall, 16), tall),
                            pl.ds(pl.multiple_of(column, 128), width),
                        ],
                        target.at[pl.ds(i * tall, tall)],
                        refs[0].at[len(copies)],
                    )
                )
        for copy in copies:
            copy.start()
        if body is not None:
            body(in_refs, out_refs)
        for copy in copies:
            copy.wait()

    out_shape = tuple(pltpu.VMEM(shape, dtype) for shape, dtype in outs)
    out_shape += tuple(pltpu.VMEM((height, width), BF16) for _, height, width, _, _ in fetches)
    return pl.pallas_call(
        kernel,
        out_shape=out_shape,
        in_specs=[VMEM] * n_in + [ANY] * (n_fetch + len(deps)),
        out_specs=(VMEM,) * (n_out + n_fetch),
        scratch_shapes=[pltpu.SemaphoreType.DMA((n_sems,))] if n_sems else [],
        compiler_params=pltpu.CompilerParams(vmem_limit_bytes=3 << 20),
        cost_estimate=COST,
        name=name,
    )(*ins, *(in_hbm(weight) for weight, *_ in fetches), *deps)


def gate_up_body(refs, out_refs):
    x_ref, gate_ref, up_ref = refs
    (out_ref,) = out_refs
    width = gate_ref.shape[1]
    x = x_ref[...]
    for base, weight in ((0, gate_ref), (width, up_ref)):
        for c in range(0, width, 256):
            got = jnp.dot(x, weight[:, c : c + 256], preferred_element_type=F32)
            out_ref[:, base + c : base + c + 256] = got.astype(out_ref.dtype)


def down_body(refs, out_refs):
    *so_far, own_ref, other_ref, w_own, w_other = refs
    for c in range(0, w_own.shape[1], 256):
        got = jnp.dot(own_ref[...], w_own[:, c : c + 256], preferred_element_type=F32)
        got += jnp.dot(other_ref[...], w_other[:, c : c + 256], preferred_element_type=F32)
        for ref in so_far:
            got += ref[:, c : c + 256]
        part = got.shape[0] // len(out_refs)
        for k, ref in enumerate(out_refs):
            ref[:, c : c + 256] = got[k * part : (k + 1) * part].astype(ref.dtype)


def plain(tokens, gate_weight, up_weight, down_weight):
    width = gate_weight.shape[1]
    piece = lax.all_gather(tokens, "ffn", axis=0, tiled=True)
    gate_part = jnp.dot(piece, gate_weight, preferred_element_type=F32)
    up_part = jnp.dot(piece, up_weight, preferred_element_type=F32)
    summed = lax.psum(jnp.concatenate([gate_part, up_part], axis=1), "mp")
    hidden = (jax.nn.silu(summed[:, :width]) * summed[:, width:]).astype(BF16)
    total = lax.psum_scatter(
        jnp.dot(hidden, down_weight, preferred_element_type=F32), "ffn", scatter_dimension=0, tiled=True
    )
    return total.astype(BF16)


def ringed(n_ffn, n_mp, tokens, gate_weight, up_weight, down_weight):
    depth, columns = gate_weight.shape[0], down_weight.shape[1]
    rows = tokens.shape[0] * n_ffn
    half = gate_weight.shape[1] // 2
    first = (half // 256 + 1) // 2 * 256
    chunks = [(0, first), (first, half - first)]

    def shift(array, k):
        return lax.ppermute(array, "ffn", [(i, (i + k) % n_ffn) for i in range(n_ffn)])

    def wide(weight, chunk, mine):
        at, width = chunks[chunk]
        return weight, depth, width, lambda core: (0, (core if mine else 1 - core) * half + at), 4

    def tall(chunk, mine):
        at, height = chunks[chunk]
        return down_weight, height, columns, lambda core: ((core if mine else 1 - core) * half + at, 0), 4

    def sums(chunk, dtype):
        return (rows, 2 * chunks[chunk][1]), dtype

    def core_swap(array):
        return lax.ppermute(array, "mp", flip(n_mp, 1))

    def cross(array):
        return lax.ppermute(array, "mp", flip(n_mp, 2))

    def hidden_of(total, crossed):
        width = total.shape[1] // 2
        total = total + crossed.astype(F32)
        return (jax.nn.silu(total[:, :width]) * total[:, width:]).astype(BF16)

    gathered = [tokens] + [shift(tokens, k) for k in range(1, n_ffn)]
    g1s, u1s, g1k = step(
        "fetch", None, [], [], [wide(gate_weight, 0, False), wide(up_weight, 0, False), wide(gate_weight, 0, True)]
    )
    x = jnp.concatenate(gathered, axis=0)
    send1, u1k = step("send_0", gate_up_body, [x, g1s, u1s], [sums(0, BF16)], [wide(up_weight, 0, True)])
    got1 = core_swap(send1)
    keep1, g2s, u2s = step(
        "keep_0",
        gate_up_body,
        [x, g1k, u1k],
        [sums(0, F32)],
        [wide(gate_weight, 1, False), wide(up_weight, 1, False)],
    )
    sum1 = keep1 + got1.astype(F32)
    out1 = sum1.astype(BF16)
    crossed1 = cross(out1)
    send2, g2k, u2k = step(
        "send_1",
        gate_up_body,
        [x, g2s, u2s],
        [sums(1, BF16)],
        [wide(gate_weight, 1, True), wide(up_weight, 1, True)],
        [out1],
    )
    got2 = core_swap(send2)
    keep2, d1k = step("keep_1", gate_up_body, [x, g2k, u2k], [sums(1, F32)], [tall(0, True)])
    sum2 = keep2 + got2.astype(F32)
    out2 = sum2.astype(BF16)
    crossed2 = cross(out2)
    h1 = hidden_of(sum1, crossed1)
    (d1s,) = step("fetch_down", None, [], [], [tall(0, False)], [out2])
    h1_other = core_swap(h1)
    so_far, d2k, d2s = step(
        "down_0",
        down_body,
        [h1, h1_other, d1k, d1s],
        [((rows, columns), F32)],
        [tall(1, True), tall(1, False)],
    )
    h2 = hidden_of(sum2, crossed2)
    h2_other = core_swap(h2)
    part = (tokens.shape[0], columns)
    own, *sends = step(
        "down_1",
        down_body,
        [so_far, h2, h2_other, d2k, d2s],
        [(part, F32)] + [(part, BF16)] * (n_ffn - 1),
        [],
    )
    for k, send in enumerate(sends, 1):
        own = own + shift(send, n_ffn - k).astype(F32)
    return own.astype(BF16)


def solution(mesh):
    n_ffn, n_mp = mesh.shape["ffn"], mesh.shape["mp"]

    def per_device(tokens, gate_weight, up_weight, down_weight):
        fits = n_mp == 4 and n_ffn <= 4 and gate_weight.shape[1] % 1024 == 512
        if fits and tokens.shape[0] == 8:
            return ringed(n_ffn, n_mp, tokens, gate_weight, up_weight, down_weight)
        return plain(tokens, gate_weight, up_weight, down_weight)

    in_specs = (P(("groups", "ffn"), "mp"), P("mp", "ffn"), P("mp", "ffn"), P("ffn", "mp"))
    out_specs = P(("groups", "ffn"), "mp")
    return jax.shard_map(
        per_device, mesh=mesh, in_specs=in_specs, out_specs=out_specs, check_vma=False
    )
```

```python
import jax
import jax.numpy as jnp
from jax import lax
from jax.experimental import pallas as pl
from jax.experimental.pallas import tpu as pltpu
from jax.sharding import PartitionSpec as P

BF16 = jnp.bfloat16
F32 = jnp.float32
VMEM = pl.BlockSpec(memory_space=pltpu.VMEM)
ANY = pl.BlockSpec(memory_space=pl.ANY)
COST = pl.CostEstimate(flops=1000, bytes_accessed=1000, transcendentals=0)


def in_hbm(array):
    return pltpu.with_memory_space_constraint(array, pltpu.HBM)


def flip(size, bit):
    return [(i, i ^ bit) for i in range(size)]


def step(name, body, ins, outs, fetches, deps=()):
    n_in, n_out, n_fetch = len(ins), len(outs), len(fetches)
    n_sems = sum(pieces for *_, pieces in fetches)

    def kernel(*refs):
        in_refs, refs = refs[:n_in], refs[n_in:]
        sources, refs = refs[:n_fetch], refs[n_fetch + len(deps) :]
        out_refs, refs = refs[:n_out], refs[n_out:]
        targets, refs = refs[:n_fetch], refs[n_fetch:]
        core = lax.rem(lax.axis_index("mp"), 2)
        copies = []
        for (_, height, width, place, pieces), source, target in zip(fetches, sources, targets):
            row, column = place(core)
            tall = height // pieces
            for i in range(pieces):
                copies.append(
                    pltpu.make_async_copy(
                        source.at[
                            pl.ds(pl.multiple_of(row + i * tall, 16), tall),
                            pl.ds(pl.multiple_of(column, 128), width),
                        ],
                        target.at[pl.ds(i * tall, tall)],
                        refs[0].at[len(copies)],
                    )
                )
        for copy in copies:
            copy.start()
        if body is not None:
            body(in_refs, out_refs)
        for copy in copies:
            copy.wait()

    out_shape = tuple(pltpu.VMEM(shape, dtype) for shape, dtype in outs)
    out_shape += tuple(pltpu.VMEM((height, width), BF16) for _, height, width, _, _ in fetches)
    return pl.pallas_call(
        kernel,
        out_shape=out_shape,
        in_specs=[VMEM] * n_in + [ANY] * (n_fetch + len(deps)),
        out_specs=(VMEM,) * (n_out + n_fetch),
        scratch_shapes=[pltpu.SemaphoreType.DMA((n_sems,))] if n_sems else [],
        compiler_params=pltpu.CompilerParams(vmem_limit_bytes=3 << 20),
        cost_estimate=COST,
        name=name,
    )(*ins, *(in_hbm(weight) for weight, *_ in fetches), *deps)


def tiled(width, most=1024):
    return max(t for t in range(128, most + 1, 128) if width % t == 0)


def each_tile(width, size, body):
    lax.fori_loop(0, width // size, lambda i, _: (body(pl.multiple_of(i * size, 128)), 0)[1], 0)


def gate_up_body(refs, out_refs):
    x_ref, gate_ref, up_ref = refs
    (out_ref,) = out_refs
    width = gate_ref.shape[1]
    size = tiled(width)
    for base, weight in ((0, gate_ref), (width, up_ref)):

        def one(at, base=base, weight=weight):
            got = jnp.dot(x_ref[...], weight[:, pl.ds(at, size)], preferred_element_type=F32)
            out_ref[:, pl.ds(pl.multiple_of(base + at, 128), size)] = got.astype(out_ref.dtype)

        each_tile(width, size, one)


def down_body(refs, out_refs):
    *so_far, own_ref, other_ref, w_own, w_other = refs
    size = 512

    def one(at):
        span = pl.ds(at, size)
        got = jnp.dot(own_ref[...], w_own[:, span], preferred_element_type=F32)
        got += jnp.dot(other_ref[...], w_other[:, span], preferred_element_type=F32)
        for ref in so_far:
            got += ref[:, span]
        part = got.shape[0] // len(out_refs)
        for k, ref in enumerate(out_refs):
            ref[:, span] = got[k * part : (k + 1) * part].astype(ref.dtype)

    each_tile(w_own.shape[1], size, one)


def copy_body(refs, out_refs):
    out_refs[0][...] = refs[0][...]


def hidden_body(refs, out_refs):
    total_ref, crossed_ref = refs
    width = total_ref.shape[1] // 2
    total = total_ref[...] + crossed_ref[...].astype(F32)
    gate = total[:, :width]
    out_refs[0][...] = (gate / (1 + jnp.exp(-gate)) * total[:, width:]).astype(BF16)


def plain(tokens, gate_weight, up_weight, down_weight):
    width = gate_weight.shape[1]
    piece = lax.all_gather(tokens, "ffn", axis=0, tiled=True)
    gate_part = jnp.dot(piece, gate_weight, preferred_element_type=F32)
    up_part = jnp.dot(piece, up_weight, preferred_element_type=F32)
    summed = lax.psum(jnp.concatenate([gate_part, up_part], axis=1), "mp")
    hidden = (jax.nn.silu(summed[:, :width]) * summed[:, width:]).astype(BF16)
    total = lax.psum_scatter(
        jnp.dot(hidden, down_weight, preferred_element_type=F32), "ffn", scatter_dimension=0, tiled=True
    )
    return total.astype(BF16)


def ringed(n_ffn, n_mp, tokens, gate_weight, up_weight, down_weight):
    depth, columns = gate_weight.shape[0], down_weight.shape[1]
    rows = tokens.shape[0] * n_ffn
    half = gate_weight.shape[1] // 2
    first = (half // 256 + 1) // 2 * 256
    chunks = [(0, first), (first, half - first)]

    def shift(array, k):
        return lax.ppermute(array, "ffn", [(i, (i + k) % n_ffn) for i in range(n_ffn)])

    def wide(weight, chunk, mine):
        at, width = chunks[chunk]
        return weight, depth, width, lambda core: (0, (core if mine else 1 - core) * half + at), 4

    def tall(chunk, mine):
        at, height = chunks[chunk]
        return down_weight, height, columns, lambda core: ((core if mine else 1 - core) * half + at, 0), 4

    def sums(chunk, dtype):
        return (rows, 2 * chunks[chunk][1]), dtype

    def core_swap(array):
        return lax.ppermute(array, "mp", flip(n_mp, 1))

    def cross(array):
        return lax.ppermute(array, "mp", flip(n_mp, 2))

    def hidden_of(total, crossed, dep):
        shape = (rows, total.shape[1] // 2)
        return step("hidden", hidden_body, [total, crossed], [(shape, BF16)], [], [dep])[0]

    tokens, g1s = step(
        "fetch_0", copy_body, [tokens], [(tokens.shape, BF16)], [wide(gate_weight, 0, False)]
    )
    gathered = [tokens] + [shift(tokens, k) for k in range(1, n_ffn)]
    u1s, g1k = step(
        "fetch_1", None, [], [], [wide(up_weight, 0, False), wide(gate_weight, 0, True)], [g1s]
    )
    x = jnp.concatenate(gathered, axis=0)
    send1, u1k = step("send_0", gate_up_body, [x, g1s, u1s], [sums(0, BF16)], [wide(up_weight, 0, True)])
    got1 = core_swap(send1)
    keep1, g2s, u2s = step(
        "keep_0",
        gate_up_body,
        [x, g1k, u1k],
        [sums(0, F32)],
        [wide(gate_weight, 1, False), wide(up_weight, 1, False)],
    )
    sum1 = keep1 + got1.astype(F32)
    out1 = sum1.astype(BF16)
    crossed1 = cross(out1)
    send2, g2k, u2k = step(
        "send_1",
        gate_up_body,
        [x, g2s, u2s],
        [sums(1, BF16)],
        [wide(gate_weight, 1, True), wide(up_weight, 1, True)],
        [out1],
    )
    got2 = core_swap(send2)
    keep2, d1k = step("keep_1", gate_up_body, [x, g2k, u2k], [sums(1, F32)], [tall(0, True)])
    sum2 = keep2 + got2.astype(F32)
    out2 = sum2.astype(BF16)
    crossed2 = cross(out2)
    (d1s,) = step("fetch_down", None, [], [], [tall(0, False)], [out2])
    h1 = hidden_of(sum1, crossed1, d1s)
    h1_other = core_swap(h1)
    so_far, d2k, d2s = step(
        "down_0",
        down_body,
        [h1, h1_other, d1k, d1s],
        [((rows, columns), F32)],
        [tall(1, True), tall(1, False)],
    )
    h2 = hidden_of(sum2, crossed2, so_far)
    h2_other = core_swap(h2)
    part = (tokens.shape[0], columns)
    own, *sends = step(
        "down_1",
        down_body,
        [so_far, h2, h2_other, d2k, d2s],
        [(part, F32)] + [(part, BF16)] * (n_ffn - 1),
        [],
    )
    for k, send in enumerate(sends, 1):
        own = own + shift(send, n_ffn - k).astype(F32)
    return own.astype(BF16)


def solution(mesh):
    n_ffn, n_mp = mesh.shape["ffn"], mesh.shape["mp"]

    def per_device(tokens, gate_weight, up_weight, down_weight):
        fits = n_mp == 4 and n_ffn <= 4 and gate_weight.shape[1] % 1024 == 512
        if fits and tokens.shape[0] == 8:
            return ringed(n_ffn, n_mp, tokens, gate_weight, up_weight, down_weight)
        return plain(tokens, gate_weight, up_weight, down_weight)

    in_specs = (P(("groups", "ffn"), "mp"), P("mp", "ffn"), P("mp", "ffn"), P("ffn", "mp"))
    out_specs = P(("groups", "ffn"), "mp")
    return jax.shard_map(
        per_device, mesh=mesh, in_specs=in_specs, out_specs=out_specs, check_vma=False
    )
```

```python
import jax
import jax.numpy as jnp
from jax import lax
from jax.experimental import pallas as pl
from jax.experimental.pallas import tpu as pltpu
from jax.sharding import PartitionSpec as P

BF16 = jnp.bfloat16
F32 = jnp.float32
VMEM = pl.BlockSpec(memory_space=pltpu.VMEM)
ANY = pl.BlockSpec(memory_space=pl.ANY)
COST = pl.CostEstimate(flops=1000, bytes_accessed=1000, transcendentals=0)


def in_hbm(array):
    return pltpu.with_memory_space_constraint(array, pltpu.HBM)


def flip(size, bit):
    return [(i, i ^ bit) for i in range(size)]


def step(name, body, ins, outs, fetches, deps=()):
    n_in, n_out, n_fetch = len(ins), len(outs), len(fetches)
    n_sems = sum(pieces for *_, pieces in fetches)

    def kernel(*refs):
        in_refs, refs = refs[:n_in], refs[n_in:]
        sources, refs = refs[:n_fetch], refs[n_fetch + len(deps) :]
        out_refs, refs = refs[:n_out], refs[n_out:]
        targets, refs = refs[:n_fetch], refs[n_fetch:]
        core = lax.rem(lax.axis_index("mp"), 2)
        copies = []
        for (_, height, width, place, pieces), source, target in zip(fetches, sources, targets):
            row, column = place(core)
            tall = height // pieces
            for i in range(pieces):
                copies.append(
                    pltpu.make_async_copy(
                        source.at[
                            pl.ds(pl.multiple_of(row + i * tall, 16), tall),
                            pl.ds(pl.multiple_of(column, 128), width),
                        ],
                        target.at[pl.ds(i * tall, tall)],
                        refs[0].at[len(copies)],
                    )
                )
        for copy in copies:
            copy.start()
        if body is not None:
            body(in_refs, out_refs)
        for copy in copies:
            copy.wait()

    out_shape = tuple(pltpu.VMEM(shape, dtype) for shape, dtype in outs)
    out_shape += tuple(pltpu.VMEM((height, width), BF16) for _, height, width, _, _ in fetches)
    return pl.pallas_call(
        kernel,
        out_shape=out_shape,
        in_specs=[VMEM] * n_in + [ANY] * (n_fetch + len(deps)),
        out_specs=(VMEM,) * (n_out + n_fetch),
        scratch_shapes=[pltpu.SemaphoreType.DMA((n_sems,))] if n_sems else [],
        compiler_params=pltpu.CompilerParams(vmem_limit_bytes=3 << 20),
        cost_estimate=COST,
        name=name,
    )(*ins, *(in_hbm(weight) for weight, *_ in fetches), *deps)


def tiled(width, most=1024):
    return max(t for t in range(128, most + 1, 128) if width % t == 0)


def each_tile(width, size, body):
    lax.fori_loop(0, width // size, lambda i, _: (body(pl.multiple_of(i * size, 128)), 0)[1], 0)


def gate_up_body(refs, out_refs):
    x_ref, gate_ref, up_ref = refs
    (out_ref,) = out_refs
    width = gate_ref.shape[1]
    size = tiled(width)
    for base, weight in ((0, gate_ref), (width, up_ref)):

        def one(at, base=base, weight=weight):
            got = jnp.dot(x_ref[...], weight[:, pl.ds(at, size)], preferred_element_type=F32)
            out_ref[:, pl.ds(pl.multiple_of(base + at, 128), size)] = got.astype(out_ref.dtype)

        each_tile(width, size, one)


def down_body(refs, out_refs):
    *so_far, own_ref, other_ref, w_own, w_other = refs
    size = 512

    def one(at):
        span = pl.ds(at, size)
        got = jnp.dot(own_ref[...], w_own[:, span], preferred_element_type=F32)
        got += jnp.dot(other_ref[...], w_other[:, span], preferred_element_type=F32)
        for ref in so_far:
            got += ref[:, span]
        part = got.shape[0] // len(out_refs)
        for k, ref in enumerate(out_refs):
            ref[:, span] = got[k * part : (k + 1) * part].astype(ref.dtype)

    each_tile(w_own.shape[1], size, one)


def sum_body(refs, out_refs):
    keep_ref, got_ref = refs
    total = keep_ref[...] + got_ref[...].astype(F32)
    out_refs[0][...] = total
    out_refs[1][...] = total.astype(BF16)


def copy_body(refs, out_refs):
    out_refs[0][...] = refs[0][...]


def join_body(refs, out_refs):
    both = [ref[...].astype(F32) for ref in refs]
    out_refs[0][...] = jnp.concatenate(both, axis=0).astype(BF16)


def hidden_body(refs, out_refs):
    total_ref, crossed_ref = refs
    width = total_ref.shape[1] // 2
    total = total_ref[...] + crossed_ref[...].astype(F32)
    gate = total[:, :width]
    out_refs[0][...] = (gate / (1 + jnp.exp(-gate)) * total[:, width:]).astype(BF16)


def plain(tokens, gate_weight, up_weight, down_weight):
    width = gate_weight.shape[1]
    piece = lax.all_gather(tokens, "ffn", axis=0, tiled=True)
    gate_part = jnp.dot(piece, gate_weight, preferred_element_type=F32)
    up_part = jnp.dot(piece, up_weight, preferred_element_type=F32)
    summed = lax.psum(jnp.concatenate([gate_part, up_part], axis=1), "mp")
    hidden = (jax.nn.silu(summed[:, :width]) * summed[:, width:]).astype(BF16)
    total = lax.psum_scatter(
        jnp.dot(hidden, down_weight, preferred_element_type=F32), "ffn", scatter_dimension=0, tiled=True
    )
    return total.astype(BF16)


def ringed(n_ffn, n_mp, tokens, gate_weight, up_weight, down_weight):
    depth, columns = gate_weight.shape[0], down_weight.shape[1]
    rows = tokens.shape[0] * n_ffn
    half = gate_weight.shape[1] // 2
    first = (half // 256 + 1) // 2 * 256
    chunks = [(0, first), (first, half - first)]

    def start_of(chunk, mine):
        return lambda core: (core if mine else 1 - core) * half + chunks[chunk][0]

    def wide(weight, chunk, mine):
        return weight, depth, chunks[chunk][1], lambda core: (0, start_of(chunk, mine)(core)), 4

    def tall(chunk, mine):
        return down_weight, chunks[chunk][1], columns, lambda core: (start_of(chunk, mine)(core), 0), 4

    def gate_up(name, chunk, mine, blocks, fetches, deps=()):
        shape = (rows, 2 * chunks[chunk][1])
        return step(name, gate_up_body, [x, *blocks], [(shape, F32 if mine else BF16)], fetches, deps)

    def core_swap(array):
        return lax.ppermute(array, "mp", flip(n_mp, 1))

    def cross(array):
        return lax.ppermute(array, "mp", flip(n_mp, 2))

    def sum_of(keep, got, deps=()):
        return step("sum", sum_body, [keep, got], [(keep.shape, F32), (keep.shape, BF16)], [], deps)

    def hidden_of(total, crossed, deps=()):
        shape = (rows, total.shape[1] // 2)
        return step("hidden", hidden_body, [total, crossed], [(shape, BF16)], [], deps)[0]

    def join(array, other, dep):
        shape = (2 * array.shape[0], depth)
        return step("join", join_body, [array, other], [(shape, BF16)], [], [dep])[0]

    gate, up = gate_weight, up_weight
    other = lax.ppermute(tokens, "ffn", flip(n_ffn, 2))
    (g1s,) = step("fetch_0", None, [], [], [wide(gate, 0, False)])
    x = join(tokens, other, g1s)
    other = lax.ppermute(x, "ffn", flip(n_ffn, 1))
    u1s, g1k = step("fetch_1", None, [], [], [wide(up, 0, False), wide(gate, 0, True)], [x])
    x = join(x, other, g1k)
    send1, u1k = gate_up("send_0", 0, False, [g1s, u1s], [wide(up, 0, True)])
    got1 = core_swap(send1)
    keep1, g2s, u2s = gate_up("keep_0", 0, True, [g1k, u1k], [wide(gate, 1, False), wide(up, 1, False)], [send1])
    sum1, out1 = sum_of(keep1, got1)
    crossed1 = cross(out1)
    send2, g2k, u2k = gate_up("send_1", 1, False, [g2s, u2s], [wide(gate, 1, True), wide(up, 1, True)], [out1])
    got2 = core_swap(send2)
    keep2, d1k = gate_up("keep_1", 1, True, [g2k, u2k], [tall(0, True)], [send2])
    h1 = hidden_of(sum1, crossed1, [keep2])
    sum2, out2 = sum_of(keep2, got2, [h1])
    crossed2 = cross(out2)
    h1_other = core_swap(h1)
    d1s, d2k = step("fetch_down", None, [], [], [tall(0, False), tall(1, True)], [out2])
    so_far, d2s = step(
        "down_0", down_body, [h1, h1_other, d1k, d1s], [((rows, columns), F32)], [tall(1, False)]
    )
    h2 = hidden_of(sum2, crossed2, [so_far])
    h2_other = core_swap(h2)
    part = (tokens.shape[0], columns)
    own, *sends = step(
        "down_1",
        down_body,
        [so_far, h2, h2_other, d2k, d2s],
        [(part, F32)] + [(part, BF16)] * (n_ffn - 1),
        [],
    )
    for bits, send in zip((2, 1, 3), sends):
        own = own + lax.ppermute(send, "ffn", flip(n_ffn, bits)).astype(F32)
    return own.astype(BF16)


def solution(mesh):
    n_ffn, n_mp = mesh.shape["ffn"], mesh.shape["mp"]

    def per_device(tokens, gate_weight, up_weight, down_weight):
        fits = n_mp == 4 and n_ffn == 4 and gate_weight.shape[1] % 1024 == 512
        if fits and tokens.shape[0] == 8:
            return ringed(n_ffn, n_mp, tokens, gate_weight, up_weight, down_weight)
        return plain(tokens, gate_weight, up_weight, down_weight)

    in_specs = (P(("groups", "ffn"), "mp"), P("mp", "ffn"), P("mp", "ffn"), P("ffn", "mp"))
    out_specs = P(("groups", "ffn"), "mp")
    return jax.shard_map(
        per_device, mesh=mesh, in_specs=in_specs, out_specs=out_specs, check_vma=False
    )
```

```python
import jax
import jax.numpy as jnp
from jax import lax
from jax.experimental import pallas as pl
from jax.experimental.pallas import tpu as pltpu
from jax.sharding import PartitionSpec as P

BF16 = jnp.bfloat16
F32 = jnp.float32
VMEM = pl.BlockSpec(memory_space=pltpu.VMEM)
ANY = pl.BlockSpec(memory_space=pl.ANY)
COST = pl.CostEstimate(flops=1000, bytes_accessed=1000, transcendentals=0)


def in_hbm(array):
    return pltpu.with_memory_space_constraint(array, pltpu.HBM)


def flip(size, bit):
    return [(i, i ^ bit) for i in range(size)]


def step(name, body, ins, outs, fetches, deps=()):
    n_in, n_out, n_fetch = len(ins), len(outs), len(fetches)
    n_sems = sum(pieces for *_, pieces in fetches)

    def kernel(*refs):
        in_refs, refs = refs[:n_in], refs[n_in:]
        sources, refs = refs[:n_fetch], refs[n_fetch + len(deps) :]
        out_refs, refs = refs[:n_out], refs[n_out:]
        targets, refs = refs[:n_fetch], refs[n_fetch:]
        core = lax.rem(lax.axis_index("mp"), 2)
        copies = []
        for (_, height, width, place, pieces), source, target in zip(fetches, sources, targets):
            row, column = place(core)
            tall = height // pieces
            for i in range(pieces):
                copies.append(
                    pltpu.make_async_copy(
                        source.at[
                            pl.ds(pl.multiple_of(row + i * tall, 16), tall),
                            pl.ds(pl.multiple_of(column, 128), width),
                        ],
                        target.at[pl.ds(i * tall, tall)],
                        refs[0].at[len(copies)],
                    )
                )
        for copy in copies:
            copy.start()
        if body is not None:
            body(in_refs, out_refs)
        for copy in copies:
            copy.wait()

    out_shape = tuple(pltpu.VMEM(shape, dtype) for shape, dtype in outs)
    out_shape += tuple(pltpu.VMEM((height, width), BF16) for _, height, width, _, _ in fetches)
    return pl.pallas_call(
        kernel,
        out_shape=out_shape,
        in_specs=[VMEM] * n_in + [ANY] * (n_fetch + len(deps)),
        out_specs=(VMEM,) * (n_out + n_fetch),
        scratch_shapes=[pltpu.SemaphoreType.DMA((n_sems,))] if n_sems else [],
        compiler_params=pltpu.CompilerParams(vmem_limit_bytes=3 << 20),
        cost_estimate=COST,
        name=name,
    )(*ins, *(in_hbm(weight) for weight, *_ in fetches), *deps)


def tiled(width, most=768):
    return max(t for t in range(128, most + 1, 128) if width % t == 0)


def each_tile(width, size, body):
    lax.fori_loop(0, width // size, lambda i, _: (body(pl.multiple_of(i * size, 128)), 0)[1], 0)


def gate_up_body(refs, out_refs):
    x_ref, gate_ref, up_ref = refs
    (out_ref,) = out_refs
    width = gate_ref.shape[1]
    size = tiled(width)
    for base, weight in ((0, gate_ref), (width, up_ref)):

        def one(at, base=base, weight=weight):
            got = jnp.dot(x_ref[...], weight[:, pl.ds(at, size)], preferred_element_type=F32)
            out_ref[:, pl.ds(pl.multiple_of(base + at, 128), size)] = got.astype(out_ref.dtype)

        each_tile(width, size, one)


def down_body(refs, out_refs):
    *so_far, own_ref, other_ref, w_own, w_other = refs
    size = 512

    def one(at):
        span = pl.ds(at, size)
        got = jnp.dot(own_ref[...], w_own[:, span], preferred_element_type=F32)
        got += jnp.dot(other_ref[...], w_other[:, span], preferred_element_type=F32)
        for ref in so_far:
            got += ref[:, span]
        part = got.shape[0] // len(out_refs)
        for k, ref in enumerate(out_refs):
            ref[:, span] = got[k * part : (k + 1) * part].astype(ref.dtype)

    each_tile(w_own.shape[1], size, one)


def sum_body(refs, out_refs):
    keep_ref, got_ref = refs
    total = keep_ref[...] + got_ref[...].astype(F32)
    out_refs[0][...] = total
    out_refs[1][...] = total.astype(BF16)


def copy_body(refs, out_refs):
    out_refs[0][...] = refs[0][...]


def join_body(refs, out_refs):
    both = [ref[...].astype(F32) for ref in refs]
    out_refs[0][...] = jnp.concatenate(both, axis=0).astype(BF16)


def hidden_body(refs, out_refs):
    total_ref, crossed_ref = refs
    width = total_ref.shape[1] // 2
    total = total_ref[...] + crossed_ref[...].astype(F32)
    gate = total[:, :width]
    out_refs[0][...] = (gate / (1 + jnp.exp(-gate)) * total[:, width:]).astype(BF16)


def plain(tokens, gate_weight, up_weight, down_weight):
    width = gate_weight.shape[1]
    piece = lax.all_gather(tokens, "ffn", axis=0, tiled=True)
    gate_part = jnp.dot(piece, gate_weight, preferred_element_type=F32)
    up_part = jnp.dot(piece, up_weight, preferred_element_type=F32)
    summed = lax.psum(jnp.concatenate([gate_part, up_part], axis=1), "mp")
    hidden = (jax.nn.silu(summed[:, :width]) * summed[:, width:]).astype(BF16)
    total = lax.psum_scatter(
        jnp.dot(hidden, down_weight, preferred_element_type=F32), "ffn", scatter_dimension=0, tiled=True
    )
    return total.astype(BF16)


def ringed(n_ffn, n_mp, tokens, gate_weight, up_weight, down_weight):
    depth, columns = gate_weight.shape[0], down_weight.shape[1]
    rows = tokens.shape[0] * n_ffn
    half = gate_weight.shape[1] // 2
    first = half // 256 * 9 // 13 * 256
    chunks = [(0, first), (first, half - first)]

    def start_of(chunk, mine):
        return lambda core: (core if mine else 1 - core) * half + chunks[chunk][0]

    def wide(weight, chunk, mine):
        return weight, depth, chunks[chunk][1], lambda core: (0, start_of(chunk, mine)(core)), 1

    def tall(chunk, mine):
        return down_weight, chunks[chunk][1], columns, lambda core: (start_of(chunk, mine)(core), 0), 1

    def gate_up(name, chunk, mine, blocks, fetches, deps=()):
        shape = (rows, 2 * chunks[chunk][1])
        return step(name, gate_up_body, [x, *blocks], [(shape, F32 if mine else BF16)], fetches, deps)

    def core_swap(array):
        return lax.ppermute(array, "mp", flip(n_mp, 1))

    def cross(array):
        return lax.ppermute(array, "mp", flip(n_mp, 2))

    def sum_of(keep, got, deps=()):
        return step("sum", sum_body, [keep, got], [(keep.shape, F32), (keep.shape, BF16)], [], deps)

    def hidden_of(total, crossed, deps=()):
        shape = (rows, total.shape[1] // 2)
        return step("hidden", hidden_body, [total, crossed], [(shape, BF16)], [], deps)[0]

    def join(array, other, dep):
        shape = (2 * array.shape[0], depth)
        return step("join", join_body, [array, other], [(shape, BF16)], [], [dep])[0]

    gate, up = gate_weight, up_weight
    other = lax.ppermute(tokens, "ffn", flip(n_ffn, 2))
    (g1s,) = step("fetch_0", None, [], [], [wide(gate, 0, False)])
    x = join(tokens, other, g1s)
    other = lax.ppermute(x, "ffn", flip(n_ffn, 1))
    u1s, g1k = step("fetch_1", None, [], [], [wide(up, 0, False), wide(gate, 0, True)], [x])
    x = join(x, other, g1k)
    send1, u1k = gate_up("send_0", 0, False, [g1s, u1s], [wide(up, 0, True)])
    got1 = core_swap(send1)
    keep1, g2s, u2s = gate_up("keep_0", 0, True, [g1k, u1k], [wide(gate, 1, False), wide(up, 1, False)], [send1])
    sum1, out1 = sum_of(keep1, got1)
    crossed1 = cross(out1)
    send2, g2k, u2k = gate_up("send_1", 1, False, [g2s, u2s], [wide(gate, 1, True), wide(up, 1, True)], [out1])
    got2 = core_swap(send2)
    keep2, d1k = gate_up("keep_1", 1, True, [g2k, u2k], [tall(0, True)], [send2])
    h1 = hidden_of(sum1, crossed1, [keep2])
    sum2, out2 = sum_of(keep2, got2, [h1])
    crossed2 = cross(out2)
    h1_other = core_swap(h1)
    (d1s,) = step("fetch_down", None, [], [], [tall(0, False)], [out2])
    h2 = hidden_of(sum2, crossed2, [d1s])
    h2_other = core_swap(h2)
    so_far, d2k, d2s = step(
        "down_0",
        down_body,
        [h1, h1_other, d1k, d1s],
        [((rows, columns), F32)],
        [tall(1, True), tall(1, False)],
        [h2],
    )
    part = (tokens.shape[0], columns)
    own, *sends = step(
        "down_1",
        down_body,
        [so_far, h2, h2_other, d2k, d2s],
        [(part, F32)] + [(part, BF16)] * (n_ffn - 1),
        [],
    )
    for bits, send in zip((2, 1, 3), sends):
        own = own + lax.ppermute(send, "ffn", flip(n_ffn, bits)).astype(F32)
    return own.astype(BF16)


def solution(mesh):
    n_ffn, n_mp = mesh.shape["ffn"], mesh.shape["mp"]

    def per_device(tokens, gate_weight, up_weight, down_weight):
        fits = n_mp == 4 and n_ffn == 4 and gate_weight.shape[1] % 1024 == 512
        if fits and tokens.shape[0] == 8:
            return ringed(n_ffn, n_mp, tokens, gate_weight, up_weight, down_weight)
        return plain(tokens, gate_weight, up_weight, down_weight)

    in_specs = (P(("groups", "ffn"), "mp"), P("mp", "ffn"), P("mp", "ffn"), P("ffn", "mp"))
    out_specs = P(("groups", "ffn"), "mp")
    return jax.shard_map(
        per_device, mesh=mesh, in_specs=in_specs, out_specs=out_specs, check_vma=False
    )
```

```python
import jax
import jax.numpy as jnp
from jax import lax
from jax.experimental import pallas as pl
from jax.experimental.pallas import tpu as pltpu
from jax.sharding import PartitionSpec as P

BF16 = jnp.bfloat16
F32 = jnp.float32
VMEM = pl.BlockSpec(memory_space=pltpu.VMEM)
ANY = pl.BlockSpec(memory_space=pl.ANY)
COST = pl.CostEstimate(flops=1000, bytes_accessed=1000, transcendentals=0)


def in_hbm(array):
    return pltpu.with_memory_space_constraint(array, pltpu.HBM)


def flip(size, bit):
    return [(i, i ^ bit) for i in range(size)]


def step(name, body, ins, outs, fetches, deps=()):
    n_in, n_out, n_fetch = len(ins), len(outs), len(fetches)
    n_sems = sum(pieces for *_, pieces in fetches)

    def kernel(*refs):
        in_refs, refs = refs[:n_in], refs[n_in:]
        sources, refs = refs[:n_fetch], refs[n_fetch + len(deps) :]
        out_refs, refs = refs[:n_out], refs[n_out:]
        targets, refs = refs[:n_fetch], refs[n_fetch:]
        core = lax.rem(lax.axis_index("mp"), 2)
        copies = []
        for (_, height, width, place, pieces), source, target in zip(fetches, sources, targets):
            row, column = place(core)
            tall = height // pieces
            for i in range(pieces):
                copies.append(
                    pltpu.make_async_copy(
                        source.at[
                            pl.ds(pl.multiple_of(row + i * tall, 16), tall),
                            pl.ds(pl.multiple_of(column, 128), width),
                        ],
                        target.at[pl.ds(i * tall, tall)],
                        refs[0].at[len(copies)],
                    )
                )
        for copy in copies:
            copy.start()
        if body is not None:
            body(in_refs, out_refs)
        for copy in copies:
            copy.wait()

    out_shape = tuple(pltpu.VMEM(shape, dtype) for shape, dtype in outs)
    out_shape += tuple(pltpu.VMEM((height, width), BF16) for _, height, width, _, _ in fetches)
    return pl.pallas_call(
        kernel,
        out_shape=out_shape,
        in_specs=[VMEM] * n_in + [ANY] * (n_fetch + len(deps)),
        out_specs=(VMEM,) * (n_out + n_fetch),
        scratch_shapes=[pltpu.SemaphoreType.DMA((n_sems,))] if n_sems else [],
        compiler_params=pltpu.CompilerParams(vmem_limit_bytes=3 << 20),
        cost_estimate=COST,
        name=name,
    )(*ins, *(in_hbm(weight) for weight, *_ in fetches), *deps)


def tiled(width, most=1152):
    return max(t for t in range(128, most + 1, 128) if width % t == 0)


def each_tile(width, size, body):
    lax.fori_loop(0, width // size, lambda i, _: (body(pl.multiple_of(i * size, 128)), 0)[1], 0)


def gate_up_body(refs, out_refs):
    x_ref, gate_ref, up_ref = refs
    (out_ref,) = out_refs
    width = gate_ref.shape[1]
    size = tiled(width)
    for base, weight in ((0, gate_ref), (width, up_ref)):

        def one(at, base=base, weight=weight):
            got = jnp.dot(x_ref[...], weight[:, pl.ds(at, size)], preferred_element_type=F32)
            out_ref[:, pl.ds(pl.multiple_of(base + at, 128), size)] = got.astype(out_ref.dtype)

        each_tile(width, size, one)


def down_body(refs, out_refs):
    *so_far, own_ref, other_ref, w_own, w_other = refs
    size = 512

    def one(at):
        span = pl.ds(at, size)
        got = jnp.dot(own_ref[...], w_own[:, span], preferred_element_type=F32)
        got += jnp.dot(other_ref[...], w_other[:, span], preferred_element_type=F32)
        for ref in so_far:
            got += ref[:, span]
        part = got.shape[0] // len(out_refs)
        for k, ref in enumerate(out_refs):
            ref[:, span] = got[k * part : (k + 1) * part].astype(ref.dtype)

    each_tile(w_own.shape[1], size, one)


def sum_body(refs, out_refs):
    keep_ref, got_ref = refs
    total = keep_ref[...] + got_ref[...].astype(F32)
    out_refs[0][...] = total
    out_refs[1][...] = total.astype(BF16)


def copy_body(refs, out_refs):
    out_refs[0][...] = refs[0][...]


def join_body(refs, out_refs):
    both = [ref[...].astype(F32) for ref in refs]
    out_refs[0][...] = jnp.concatenate(both, axis=0).astype(BF16)


def hidden_body(refs, out_refs):
    total_ref, crossed_ref = refs
    width = total_ref.shape[1] // 2
    total = total_ref[...] + crossed_ref[...].astype(F32)
    gate = total[:, :width]
    out_refs[0][...] = (gate / (1 + jnp.exp(-gate)) * total[:, width:]).astype(BF16)


def plain(tokens, gate_weight, up_weight, down_weight):
    width = gate_weight.shape[1]
    piece = lax.all_gather(tokens, "ffn", axis=0, tiled=True)
    gate_part = jnp.dot(piece, gate_weight, preferred_element_type=F32)
    up_part = jnp.dot(piece, up_weight, preferred_element_type=F32)
    summed = lax.psum(jnp.concatenate([gate_part, up_part], axis=1), "mp")
    hidden = (jax.nn.silu(summed[:, :width]) * summed[:, width:]).astype(BF16)
    total = lax.psum_scatter(
        jnp.dot(hidden, down_weight, preferred_element_type=F32), "ffn", scatter_dimension=0, tiled=True
    )
    return total.astype(BF16)


def shared(n_groups, n_ffn, n_mp, tokens, gate_weight, up_weight, down_weight):
    depth, columns = gate_weight.shape[0], down_weight.shape[1]
    few = tokens.shape[0]
    rows = few * n_ffn * n_groups
    half = gate_weight.shape[1] // n_groups
    quarter = half // 2
    first = quarter // 128 * 9 // 13 * 128
    chunks = [(0, first), (first, quarter - first)]

    def swap(array, axis, size, bit):
        return lax.ppermute(array, axis, flip(size, bit))

    def start_of(chunk, mine, core):
        owner = core if mine else 1 - core
        return lax.axis_index("groups") * half + owner * quarter + chunks[chunk][0]

    def wide(weight, chunk, mine):
        return weight, depth, chunks[chunk][1], lambda core: (0, start_of(chunk, mine, core)), 1

    def both(chunk, mine):
        return [wide(gate_weight, chunk, mine), wide(up_weight, chunk, mine)]

    def tall(chunk):
        return [
            (down_weight, chunks[chunk][1], columns, lambda core, mine=mine: (start_of(chunk, mine, core), 0), 1)
            for mine in (True, False)
        ]

    def sums(chunk, dtype):
        return (rows, 2 * chunks[chunk][1]), dtype

    def core_swap(array):
        return swap(array, "mp", n_mp, 1)

    def cross(array):
        return swap(array, "mp", n_mp, 2)

    def sum_of(keep, got, deps=()):
        return step("sum", sum_body, [keep, got], [(keep.shape, F32), (keep.shape, BF16)], [], deps)

    def hidden_of(total, crossed, deps=()):
        shape = (rows, total.shape[1] // 2)
        return step("hidden", hidden_body, [total, crossed], [(shape, BF16)], [], deps)[0]

    def join(array, other, dep):
        shape = (2 * array.shape[0], depth)
        return step("join", join_body, [array, other], [(shape, BF16)], [], [dep])[0]

    other = swap(tokens, "ffn", n_ffn, 2)
    g1s, u1s = step("fetch_0", None, [], [], both(0, False))
    x = join(tokens, other, g1s)
    other = swap(x, "ffn", n_ffn, 1)
    g1k, u1k = step("fetch_1", None, [], [], both(0, True), [x])
    x = join(x, other, g1k)
    other = swap(x, "groups", n_groups, 1)
    g2s, u2s, g2k, u2k = step("fetch_2", None, [], [], both(1, False) + both(1, True), [x])
    x = join(x, other, g2s)
    (send1,) = step("send_0", gate_up_body, [x, g1s, u1s], [sums(0, BF16)], [])
    got1 = core_swap(send1)
    (keep1,) = step("keep_0", gate_up_body, [x, g1k, u1k], [sums(0, F32)], [], [send1])
    sum1, out1 = sum_of(keep1, got1)
    crossed1 = cross(out1)
    (send2,) = step("send_1", gate_up_body, [x, g2s, u2s], [sums(1, BF16)], [], [out1])
    got2 = core_swap(send2)
    (keep2,) = step("keep_1", gate_up_body, [x, g2k, u2k], [sums(1, F32)], [], [send2])
    sum2, out2 = sum_of(keep2, got2)
    crossed2 = cross(out2)
    d1k, d1s, d2k, d2s = step("fetch_3", None, [], [], tall(0) + tall(1), [out2])
    h1 = hidden_of(sum1, crossed1, [d1k])
    h1_other = core_swap(h1)
    h2 = hidden_of(sum2, crossed2, [h1])
    h2_other = core_swap(h2)
    (so_far,) = step("down_0", down_body, [h1, h1_other, d1k, d1s], [((rows, columns), F32)], [], [h2])
    part = (rows // 2, columns)
    own, send = step(
        "down_1", down_body, [so_far, h2, h2_other, d2k, d2s], [(part, F32), (part, BF16)], []
    )
    own = own + swap(send, "groups", n_groups, 1).astype(F32)
    few = tokens.shape[0]
    total = own[:few]
    for k, bits in ((1, 2), (2, 1), (3, 3)):
        send = own[k * few : (k + 1) * few].astype(BF16)
        total = total + swap(send, "ffn", n_ffn, bits).astype(F32)
    return total.astype(BF16)


def solution(mesh):
    n_groups, n_ffn, n_mp = mesh.shape["groups"], mesh.shape["ffn"], mesh.shape["mp"]

    def per_device(tokens, gate_weight, up_weight, down_weight):
        fits = (n_groups, n_ffn, n_mp) == (2, 4, 4) and gate_weight.shape[1] % 512 == 0
        if fits and tokens.shape[0] == 8:
            return shared(n_groups, n_ffn, n_mp, tokens, gate_weight, up_weight, down_weight)
        return plain(tokens, gate_weight, up_weight, down_weight)

    in_specs = (P(("groups", "ffn"), "mp"), P("mp", "ffn"), P("mp", "ffn"), P("ffn", "mp"))
    out_specs = P(("groups", "ffn"), "mp")
    return jax.shard_map(
        per_device, mesh=mesh, in_specs=in_specs, out_specs=out_specs, check_vma=False
    )
```

```python
import jax
import jax.numpy as jnp
from jax import lax
from jax.experimental import pallas as pl
from jax.experimental.pallas import tpu as pltpu
from jax.sharding import PartitionSpec as P

BF16 = jnp.bfloat16
F32 = jnp.float32
VMEM = pl.BlockSpec(memory_space=pltpu.VMEM)
ANY = pl.BlockSpec(memory_space=pl.ANY)
COST = pl.CostEstimate(flops=1000, bytes_accessed=1000, transcendentals=0)


def in_hbm(array):
    return pltpu.with_memory_space_constraint(array, pltpu.HBM)


def flip(size, bit):
    return [(i, i ^ bit) for i in range(size)]


def step(name, body, ins, outs, fetches, deps=()):
    n_in, n_out, n_fetch = len(ins), len(outs), len(fetches)
    n_sems = sum(pieces for *_, pieces in fetches)

    def kernel(*refs):
        in_refs, refs = refs[:n_in], refs[n_in:]
        sources, refs = refs[:n_fetch], refs[n_fetch + len(deps) :]
        out_refs, refs = refs[:n_out], refs[n_out:]
        targets, refs = refs[:n_fetch], refs[n_fetch:]
        core = lax.rem(lax.axis_index("mp"), 2)
        copies = []
        for (_, height, width, place, pieces), source, target in zip(fetches, sources, targets):
            row, column = place(core)
            tall = height // pieces
            for i in range(pieces):
                copies.append(
                    pltpu.make_async_copy(
                        source.at[
                            pl.ds(pl.multiple_of(row + i * tall, 16), tall),
                            pl.ds(pl.multiple_of(column, 128), width),
                        ],
                        target.at[pl.ds(i * tall, tall)],
                        refs[0].at[len(copies)],
                    )
                )
        for copy in copies:
            copy.start()
        if body is not None:
            body(in_refs, out_refs)
        for copy in copies:
            copy.wait()

    out_shape = tuple(pltpu.VMEM(shape, dtype) for shape, dtype in outs)
    out_shape += tuple(pltpu.VMEM((height, width), BF16) for _, height, width, _, _ in fetches)
    return pl.pallas_call(
        kernel,
        out_shape=out_shape,
        in_specs=[VMEM] * n_in + [ANY] * (n_fetch + len(deps)),
        out_specs=(VMEM,) * (n_out + n_fetch),
        scratch_shapes=[pltpu.SemaphoreType.DMA((n_sems,))] if n_sems else [],
        compiler_params=pltpu.CompilerParams(vmem_limit_bytes=3 << 20),
        cost_estimate=COST,
        name=name,
    )(*ins, *(in_hbm(weight) for weight, *_ in fetches), *deps)


def tiled(width, most=1152):
    return max(t for t in range(128, most + 1, 128) if width % t == 0)


def each_tile(width, size, body):
    lax.fori_loop(0, width // size, lambda i, _: (body(pl.multiple_of(i * size, 128)), 0)[1], 0)


def gate_up_body(refs, out_refs):
    x_ref, gate_ref, up_ref = refs
    (out_ref,) = out_refs
    width = gate_ref.shape[1]
    size = tiled(width)
    for base, weight in ((0, gate_ref), (width, up_ref)):

        def one(at, base=base, weight=weight):
            got = jnp.dot(x_ref[...], weight[:, pl.ds(at, size)], preferred_element_type=F32)
            out_ref[:, pl.ds(pl.multiple_of(base + at, 128), size)] = got.astype(out_ref.dtype)

        each_tile(width, size, one)


def down_body(refs, out_refs):
    n_pairs = len(refs) // 2
    pairs = list(zip(refs[:n_pairs], refs[n_pairs : 2 * n_pairs]))
    size = 512

    def one(at):
        span = pl.ds(at, size)
        got = sum(jnp.dot(h_ref[...], w_ref[:, span], preferred_element_type=F32) for h_ref, w_ref in pairs)
        for ref in refs[2 * n_pairs :]:
            got += ref[:, span]
        part = got.shape[0] // len(out_refs)
        for k, ref in enumerate(out_refs):
            ref[:, span] = got[k * part : (k + 1) * part].astype(ref.dtype)

    each_tile(pairs[0][1].shape[1], size, one)


def sum_body(refs, out_refs):
    keep_ref, got_ref = refs
    total = keep_ref[...] + got_ref[...].astype(F32)
    out_refs[0][...] = total
    out_refs[1][...] = total.astype(BF16)


def copy_body(refs, out_refs):
    out_refs[0][...] = refs[0][...]


def join_body(refs, out_refs):
    both = [ref[...].astype(F32) for ref in refs]
    out_refs[0][...] = jnp.concatenate(both, axis=0).astype(BF16)


def hidden_body(refs, out_refs):
    total_ref, crossed_ref = refs
    width = total_ref.shape[1] // 2
    total = total_ref[...] + crossed_ref[...].astype(F32)
    gate = total[:, :width]
    out_refs[0][...] = (gate / (1 + jnp.exp(-gate)) * total[:, width:]).astype(BF16)


def plain(tokens, gate_weight, up_weight, down_weight):
    width = gate_weight.shape[1]
    piece = lax.all_gather(tokens, "ffn", axis=0, tiled=True)
    gate_part = jnp.dot(piece, gate_weight, preferred_element_type=F32)
    up_part = jnp.dot(piece, up_weight, preferred_element_type=F32)
    summed = lax.psum(jnp.concatenate([gate_part, up_part], axis=1), "mp")
    hidden = (jax.nn.silu(summed[:, :width]) * summed[:, width:]).astype(BF16)
    total = lax.psum_scatter(
        jnp.dot(hidden, down_weight, preferred_element_type=F32), "ffn", scatter_dimension=0, tiled=True
    )
    return total.astype(BF16)


def shared(n_groups, n_ffn, n_mp, tokens, gate_weight, up_weight, down_weight):
    depth, columns = gate_weight.shape[0], down_weight.shape[1]
    few = tokens.shape[0]
    rows = few * n_ffn * n_groups
    half = gate_weight.shape[1] // n_groups
    quarter = half // 2
    first = quarter // 128 * 9 // 13 * 128
    chunks = [(0, first), (first, quarter - first)]

    def swap(array, axis, size, bit):
        return lax.ppermute(array, axis, flip(size, bit))

    def start_of(chunk, mine, core):
        owner = core if mine else 1 - core
        return lax.axis_index("groups") * half + owner * quarter + chunks[chunk][0]

    def wide(weight, chunk, mine):
        return weight, depth, chunks[chunk][1], lambda core: (0, start_of(chunk, mine, core)), 1

    def both(chunk, mine):
        return [wide(gate_weight, chunk, mine), wide(up_weight, chunk, mine)]

    def tall(chunk):
        return [
            (down_weight, chunks[chunk][1], columns, lambda core, mine=mine: (start_of(chunk, mine, core), 0), 1)
            for mine in (True, False)
        ]

    def sums(chunk, dtype):
        return (rows, 2 * chunks[chunk][1]), dtype

    def core_swap(array):
        return swap(array, "mp", n_mp, 1)

    def cross(array):
        return swap(array, "mp", n_mp, 2)

    def sum_of(keep, got, deps=()):
        return step("sum", sum_body, [keep, got], [(keep.shape, F32), (keep.shape, BF16)], [], deps)

    def hidden_of(total, crossed, deps=()):
        shape = (rows, total.shape[1] // 2)
        return step("hidden", hidden_body, [total, crossed], [(shape, BF16)], [], deps)[0]

    def join(array, other, dep):
        shape = (2 * array.shape[0], depth)
        return step("join", join_body, [array, other], [(shape, BF16)], [], [dep])[0]

    other = swap(tokens, "ffn", n_ffn, 2)
    g1s, u1s = step("fetch_0", None, [], [], both(0, False))
    x = join(tokens, other, g1s)
    other = swap(x, "ffn", n_ffn, 1)
    g1k, u1k = step("fetch_1", None, [], [], both(0, True), [x])
    x = join(x, other, g1k)
    other = swap(x, "groups", n_groups, 1)
    g2s, u2s, g2k, u2k = step("fetch_2", None, [], [], both(1, False) + both(1, True), [x])
    x = join(x, other, g2s)
    (send1,) = step("send_0", gate_up_body, [x, g1s, u1s], [sums(0, F32)], [])
    got1 = core_swap(send1)
    (keep1,) = step("keep_0", gate_up_body, [x, g1k, u1k], [sums(0, F32)], [], [send1])
    sum1, out1 = sum_of(keep1, got1)
    crossed1 = cross(out1)
    (send2,) = step("send_1", gate_up_body, [x, g2s, u2s], [sums(1, BF16)], [], [out1])
    got2 = core_swap(send2)
    (keep2,) = step("keep_1", gate_up_body, [x, g2k, u2k], [sums(1, F32)], [], [send2])
    sum2, out2 = sum_of(keep2, got2)
    crossed2 = cross(out2)
    d1k, d1s, d2k, d2s = step("fetch_3", None, [], [], tall(0) + tall(1), [out2])
    h1 = hidden_of(sum1, crossed1, [d1k])
    h1_other = core_swap(h1)
    whole, part = (rows, columns), (rows // 2, columns)
    (so_far,) = step("down_0", down_body, [h1, d1k], [(whole, F32)], [])
    h2 = hidden_of(sum2, crossed2, [so_far])
    h2_other = core_swap(h2)
    (so_far,) = step("down_1", down_body, [h1_other, d1s, so_far], [(whole, F32)], [], [h2])
    own, send = step(
        "down_2", down_body, [h2, h2_other, d2k, d2s, so_far], [(part, F32), (part, BF16)], []
    )
    own = own + swap(send, "groups", n_groups, 1).astype(F32)
    few = tokens.shape[0]
    total = own[:few]
    for k, bits in ((1, 2), (2, 1), (3, 3)):
        send = own[k * few : (k + 1) * few].astype(BF16)
        total = total + swap(send, "ffn", n_ffn, bits).astype(F32)
    return total.astype(BF16)


def solution(mesh):
    n_groups, n_ffn, n_mp = mesh.shape["groups"], mesh.shape["ffn"], mesh.shape["mp"]

    def per_device(tokens, gate_weight, up_weight, down_weight):
        fits = (n_groups, n_ffn, n_mp) == (2, 4, 4) and gate_weight.shape[1] % 512 == 0
        if fits and tokens.shape[0] == 8:
            return shared(n_groups, n_ffn, n_mp, tokens, gate_weight, up_weight, down_weight)
        return plain(tokens, gate_weight, up_weight, down_weight)

    in_specs = (P(("groups", "ffn"), "mp"), P("mp", "ffn"), P("mp", "ffn"), P("ffn", "mp"))
    out_specs = P(("groups", "ffn"), "mp")
    return jax.shard_map(
        per_device, mesh=mesh, in_specs=in_specs, out_specs=out_specs, check_vma=False
    )
```
